32 devices in a mesh: groups: 2 (over x), row: 4 (over y, core), col: 4 (over z).
Axes of the slice: x: 2, y: 2, z: 4, core: 2. Of those that a mesh axis runs over, the one named last changes fastest.
Arguments:
- positions: float32 [3, 32768], P(None, ('groups', 'row', 'col')), parts along dimension 1, may hold values from -6 to 6
- strengths: float32 [3, 32768], P(None, ('groups', 'row', 'col')), parts along dimension 1, may hold values from -6 to 6
- cores: float32 [32768], P(('groups', 'row', 'col')), parts along dimension 0, may hold values from 0.3 to 1
- order: int32 [32768], P(('groups', 'row', 'col')), parts along dimension 0, may hold values from 0 to 1023, as said below
- tile_counts: int32 [256], P(('groups', 'row', 'col')), parts along dimension 0, may hold values from 32 to 128
- pair_slots: int32 [2, 2048], P(None, ('groups', 'row', 'col')), parts along dimension 1, may hold values from 0 to 31, as said below
- pair_count: int32 [32], P(('groups', 'row', 'col')), parts along dimension 0, may hold values from 16 to 64, as said below
Outputs:
- velocity: float32 [3, 32768], P(None, ('groups', 'row', 'col')), parts along dimension 1
- stretching: float32 [3, 32768], P(None, ('groups', 'row', 'col')), parts along dimension 1
The draws below stay inside these ranges and needn't reach their ends.
There are 2 independent parts, one for each index of `groups`. The reference program is written for one: setup_inputs(seed, part) draws one part's arguments, and reference() takes and returns one part's arrays. A program takes and returns all parts, laid end to end along the dimension named above; each array names one. Nothing has to cross between parts.
Inputs may be any that keep to these rules, and one draw needn't show every extreme that they name: `order`: each device's block of 1024 entries is a permutation of 0 to 1023. `pair_slots`: row 0 is below 32, row 1 below 32; the first 8 slots of every device pair each of its own tiles with itself. `pair_count`: some device has all its slots live.
All inputs are finite; a program needn't handle non-finite values.
Results may differ from the reference program's by a relative error of at most 0.0001.
Values sent between devices are 32-bit elements; how exact they have to be, the bound alone decides.
A program may use at most 64 MiB of HBM per device.

```python
import math
import jax
import jax.numpy as jnp
from jax import lax

TILE = 128
TILES_DEV = 8
PAIRS_DEV = 64
PAIR_BLOCK = 8
GRID = 16
TILES = 128
NPART = 16384
ROW_TILES = 32
COL_TILES = 32
SLOTS = 1024
N_COL = 4


def draw_order(key, part):
    per_dev = TILES_DEV * TILE
    count = NPART // per_dev
    keys = jax.random.split(jax.random.fold_in(key, 11), count)
    perms = jax.vmap(lambda single: jax.random.permutation(single, per_dev))(keys)
    return perms.reshape(-1).astype(jnp.int32)


def draw_pair_slots(key, part):
    ncols = ROW_TILES // TILES_DEV
    slot = jnp.arange(SLOTS, dtype=jnp.int32)
    device = slot // PAIRS_DEV
    within = slot % PAIRS_DEV
    row_index = device // ncols
    col_index = device % ncols
    first = jax.random.randint(jax.random.fold_in(key, 21), (SLOTS,), 0, ROW_TILES, dtype=jnp.int32)
    second = jax.random.randint(jax.random.fold_in(key, 22), (SLOTS,), 0, COL_TILES, dtype=jnp.int32)
    diagonal = within < TILES_DEV
    first = jnp.where(diagonal, col_index * TILES_DEV + within, first)
    second = jnp.where(diagonal, row_index * TILES_DEV + within, second)
    return jnp.stack([first, second]).astype(jnp.int32)


def draw_pair_count(key, part):
    base = jax.random.randint(jax.random.fold_in(key, 31), (GRID,), PAIRS_DEV // 4, PAIRS_DEV // 2 + 1, dtype=jnp.int32)
    dense = jax.random.randint(jax.random.fold_in(key, 32), (GRID,), 0, 8, dtype=jnp.int32) == 0
    chosen = jax.random.randint(jax.random.fold_in(key, 33), (), 0, GRID, dtype=jnp.int32)
    full = dense | (jnp.arange(GRID, dtype=jnp.int32) == chosen)
    return jnp.where(full, PAIRS_DEV, base).astype(jnp.int32)


def place_ends(result, key, low, largest):
    longest = result.shape.index(max(result.shape))
    spots = []
    for shift in (0, 1):
        where = [jax.random.randint(jax.random.fold_in(key, axis), (), 0, length) for axis, length in enumerate(result.shape)]
        where[longest] = (where[longest] + shift) % result.shape[longest]
        spots.append(tuple(where))
    return result.at[spots[0]].set(low).at[spots[1]].set(largest)


def block_scale(rng, extent, cuts, low, high):
    loudness, own = 1.0, jax.random.fold_in(rng, 6)
    for dim, shards_of in cuts:
        steps = jnp.exp(jax.random.uniform(jax.random.fold_in(own, dim), (shards_of,), jnp.float32, low / len(cuts), high / len(cuts)))
        loudness = loudness * jnp.repeat(steps, extent[dim] // shards_of).reshape([-1 if axis == dim else 1 for axis in range(len(extent))])
    return loudness


def bell_draw(stream_key, shape, width, bound, cuts=(), kind=jnp.bfloat16):
    gain = block_scale(stream_key, shape, cuts, -0.22, 0.18) if cuts else 1.0
    result = jax.random.normal(stream_key, shape, jnp.float32) * width * gain
    return jnp.minimum(jnp.maximum(result, -bound), bound).astype(kind)


def setup_inputs(seed: int = 0, part: int = 0) -> dict:
    arg_keys = jax.random.split(jax.random.key(seed), 8)
    part_keys = jax.random.split(jax.random.fold_in(arg_keys[7], part), 8)
    return {
        "positions": bell_draw(part_keys[0], (3, NPART), 1.0, 6.0, ((1, 16),), jnp.float32),
        "strengths": bell_draw(part_keys[1], (3, NPART), 1.0, 6.0, ((1, 16),), jnp.float32),
        "cores": jnp.clip(jnp.exp(math.log(1.0) - 1.2039728 * jax.random.uniform(part_keys[2], (NPART,), jnp.float32) ** block_scale(part_keys[2], (NPART,), ((0, 16),), -0.2, 0.2)), 0.3, 1.0),
        "order": draw_order(jax.random.fold_in(jax.random.fold_in(arg_keys[7], part), 71), part),
        "tile_counts": place_ends(jax.random.randint(part_keys[4], (TILES,), TILE // 4, TILE + 1), jax.random.fold_in(part_keys[4], 1), TILE // 4, TILE).astype(jnp.int32),
        "pair_slots": draw_pair_slots(jax.random.fold_in(jax.random.fold_in(arg_keys[7], part), 71), part),
        "pair_count": draw_pair_count(jax.random.fold_in(jax.random.fold_in(arg_keys[7], part), 71), part),
    }


biot_factor = -1.0 / (4.0 * math.pi)

def cross_product(left, right):
    return jnp.stack([left[1] * right[2] - left[2] * right[1], left[2] * right[0] - left[0] * right[2], left[0] * right[1] - left[1] * right[0]])

def pair_terms(target, source, weight_t, weight_r):
    target_pos = target[0:3, :, :, None]
    source_pos = source[0:3, :, None, :]
    target_str = target[3:6, :, :, None]
    source_str = source[3:6, :, None, :]
    offset = target_pos - source_pos
    sigma_sq = 0.5 * (target[6][:, :, None] ** 2 + source[6][:, None, :] ** 2)
    rho_sq = (offset[0] * offset[0] + offset[1] * offset[1] + offset[2] * offset[2]) / sigma_sq
    inverse = lax.rsqrt(rho_sq + 1.0)
    inverse_sq = inverse * inverse
    inverse_five = inverse_sq * inverse_sq * inverse
    core_cube = sigma_sq * jnp.sqrt(sigma_sq)
    smooth = (rho_sq + 2.5) * inverse_five / core_cube
    gradient = -3.0 * (rho_sq + 3.5) * inverse_five * inverse_sq / (core_cube * sigma_sq)
    cross_src = cross_product(offset, source_str)
    cross_tgt = cross_product(offset, target_str)
    along_tgt = lax.optimization_barrier(jnp.sum(target_str * offset, axis=0))
    along_src = lax.optimization_barrier(jnp.sum(source_str * offset, axis=0))
    smooth_t = smooth * weight_t[:, None, None]
    grad_t = gradient * weight_t[:, None, None]
    vel_target = biot_factor * lax.optimization_barrier(jnp.sum(smooth_t * cross_src, axis=-1))
    mix_target = lax.optimization_barrier(jnp.sum(smooth_t * source_str, axis=-1))
    str_target = biot_factor * (cross_product(target[3:6], mix_target) + lax.optimization_barrier(jnp.sum(grad_t * along_tgt * cross_src, axis=-1)))
    smooth_r = smooth * weight_r[:, None, None]
    grad_r = gradient * weight_r[:, None, None]
    vel_source = -biot_factor * lax.optimization_barrier(jnp.sum(smooth_r * cross_tgt, axis=-2))
    mix_source = lax.optimization_barrier(jnp.sum(smooth_r * target_str, axis=-2))
    str_source = biot_factor * (-cross_product(mix_source, source[3:6]) + lax.optimization_barrier(jnp.sum(grad_r * along_src * cross_tgt, axis=-2)))
    return (jnp.concatenate([vel_target, str_target], axis=0), jnp.concatenate([vel_source, str_source], axis=0))

def reference(positions, strengths, cores, order, tile_counts, pair_slots, pair_count):
    per_dev = TILES_DEV * TILE
    spots = jnp.arange(NPART, dtype=jnp.int32)
    index = order + spots // per_dev * per_dev
    live = (spots % TILE < tile_counts[spots // TILE]).astype(jnp.float32)
    packed = jnp.concatenate([positions[:, index], strengths[:, index] * live, cores[index][None, :]], axis=0)
    tiles = packed.reshape(7, TILES, TILE)
    slot = jnp.arange(SLOTS, dtype=jnp.int32)
    device = slot // PAIRS_DEV
    row_index = device // N_COL
    col_index = device % N_COL
    first = pair_slots[0]
    second = pair_slots[1]
    target_tile = row_index * ROW_TILES + first
    source_tile = (second // TILES_DEV * N_COL + col_index) * TILES_DEV + second % TILES_DEV
    alive = (slot % PAIRS_DEV < pair_count[device]).astype(jnp.float32)
    react = alive * (target_tile != source_tile).astype(jnp.float32)
    blocks = SLOTS // PAIR_BLOCK

    def step(total, items):
        tgt_idx, src_idx, weight_t, weight_r = items
        tgt_terms, src_terms = pair_terms(tiles[:, tgt_idx], tiles[:, src_idx], weight_t, weight_r)
        total = total.at[:, tgt_idx].add(tgt_terms)
        total = total.at[:, src_idx].add(src_terms)
        return (total, None)
    items = (target_tile.reshape(blocks, PAIR_BLOCK), source_tile.reshape(blocks, PAIR_BLOCK), alive.reshape(blocks, PAIR_BLOCK), react.reshape(blocks, PAIR_BLOCK))
    total, _ = lax.scan(step, jnp.zeros((6, TILES, TILE), jnp.float32), items)
    total = total.reshape(6, NPART) * live
    return (total[0:3], total[3:6])
```

```python
import functools
import math

import jax
import jax.numpy as jnp
from jax import lax
from jax.experimental import pallas as pl
from jax.experimental.pallas import tpu as pltpu
from jax.sharding import PartitionSpec as P

TILE = 128
MESH = pl.DeviceIdType.MESH
VMEM = pl.BlockSpec(memory_space=pltpu.VMEM)
SMEM = pl.BlockSpec(memory_space=pltpu.SMEM)
UNROLL = 2
CHUNK = 16

biot_factor = -1.0 / (4.0 * math.pi)


def peers(nrows, ncols):
    return [("col", k) for k in range(1, ncols)] + [("row", k) for k in range(1, nrows)]


def greet(nrows, ncols):
    barrier = pltpu.get_barrier_semaphore()
    for axis, k in peers(nrows, ncols):
        size = ncols if axis == "col" else nrows
        other = lax.rem(lax.axis_index(axis) + k, size)
        pl.semaphore_signal(barrier, inc=1, device_id={axis: other}, device_id_type=MESH)
    return barrier


def gather_kernel(nrows, ncols, tiles, pos, strg, cores, order, counts, row_out, col_out, raw, mine, send, recv):
    barrier = greet(nrows, ncols)
    row = lax.axis_index("row")
    col = lax.axis_index("col")
    lane = lax.broadcasted_iota(jnp.int32, (8, TILE), 1)
    sub = lax.broadcasted_iota(jnp.int32, (8, TILE), 0)
    for t in range(tiles):
        part = slice(t * TILE, (t + 1) * TILE)
        raw[t] = jnp.zeros((8, TILE), jnp.float32)
        raw[t, 0:3, :] = pos[:, part]
        raw[t, 3:6, :] = strg[:, part]
        raw[t, 6:7, :] = cores[t : t + 1, :]
    for t in range(tiles):
        spot = jnp.broadcast_to(order[t : t + 1, :], (8, TILE))
        inner = spot % TILE
        outer = spot // TILE
        found = jnp.zeros((8, TILE), jnp.float32)
        for s in range(tiles):
            found = jnp.where(outer == s, jnp.take_along_axis(raw[s], inner, axis=1), found)
        keep = (lane < counts[t]) | (sub < 3) | (sub > 5)
        mine[t] = jnp.where(keep, found, 0.0)
    pl.semaphore_wait(barrier, nrows + ncols - 2)
    copies = []
    for n, (axis, k) in enumerate(peers(nrows, ncols)):
        size, me = (ncols, col) if axis == "col" else (nrows, row)
        dest = row_out if axis == "col" else col_out
        copy = pltpu.make_async_remote_copy(
            src_ref=mine,
            dst_ref=dest.at[me],
            send_sem=send.at[n],
            recv_sem=recv.at[n],
            device_id={axis: lax.rem(me + k, size)},
            device_id_type=MESH,
        )
        copy.start()
        copies.append(copy)
    row_out[col] = mine[...]
    col_out[row] = mine[...]
    for copy in copies:
        copy.wait()


def split(value):
    high = value.astype(jnp.bfloat16)
    return high, (value - high.astype(jnp.float32)).astype(jnp.bfloat16)


def pair_kernel(nrows, ncols, tiles, slots, count, row_blk, col_blk, row_out, col_out,
                across, row_w, col_w, row_acc, col_acc, tgt_buf, src_buf):
    row = lax.axis_index("row")
    col = lax.axis_index("col")
    row_acc[...] = jnp.zeros_like(row_acc)
    col_acc[...] = jnp.zeros_like(col_acc)

    def features(block):
        x = block[0:3]
        a = block[3:6]
        b = [x[1] * a[2] - x[2] * a[1], x[2] * a[0] - x[0] * a[2], x[0] * a[1] - x[1] * a[0]]
        vectors = jnp.concatenate([a] + [v[None, :] for v in b], axis=0)
        high = vectors.astype(jnp.bfloat16).astype(jnp.float32)
        zeros = jnp.zeros((4, TILE), jnp.float32)
        both = jnp.concatenate([high, vectors - high, zeros], axis=0).astype(jnp.bfloat16)
        return jnp.concatenate([both, both], axis=1)

    def prepare_row(t, _):
        block = row_blk[t]
        across[t] = block.T
        row_w[t] = features(block)
        return 0

    def prepare_col(t, _):
        col_w[t] = features(col_blk[t])
        return 0

    lax.fori_loop(0, row_blk.shape[0], prepare_row, 0)
    lax.fori_loop(0, col_blk.shape[0], prepare_col, 0)

    def visit(step, _):
        for u in range(UNROLL):
            s = step * UNROLL + u
            ti = slots[0, s]
            sj = slots[1, s]
            alive = jnp.where(s < count[0], 1.0, 0.0)
            gi = row * (ncols * tiles) + ti
            gj = ((sj // tiles) * ncols + col) * tiles + sj % tiles
            react = jnp.where(gi != gj, alive, 0.0)
            src = col_blk[sj]
            xj = [src[k : k + 1, :] for k in range(7)]
            hj = 0.5 * xj[6] * xj[6]
            for c in range(TILE // CHUNK):
                at = slice(c * CHUNK, (c + 1) * CHUNK)
                at2 = slice(TILE + c * CHUNK, TILE + (c + 1) * CHUNK)
                tgt = across[ti, at, :]
                xi = [tgt[:, k : k + 1] for k in range(7)]
                hi = 0.5 * xi[6] * xi[6]
                dx = xi[0] - xj[0]
                dy = xi[1] - xj[1]
                dz = xi[2] - xj[2]
                s2 = hi + hj
                d = dx * dx + dy * dy + dz * dz + s2
                inv = lax.rsqrt(d)
                inv2 = inv * inv
                inv3 = inv2 * inv
                w = s2 * (inv3 * inv2)
                q = inv3 + 1.5 * w
                f = (q + w) * inv2
                g = f * (xi[3] * dx + xi[4] * dy + xi[5] * dz)
                h = f * (xj[3] * dx + xj[4] * dy + xj[5] * dz)
                q1, q2 = split(q)
                g1, g2 = split(g)
                h1, h2 = split(h)
                tgt_buf[u, at, 0:TILE] = q1
                tgt_buf[u, at, TILE:] = q2
                tgt_buf[u, at2, 0:TILE] = g1
                tgt_buf[u, at2, TILE:] = g2
                src_buf[u, at, 0:TILE] = q1
                src_buf[u, at, TILE:] = h1
                src_buf[u, at2, 0:TILE] = q2
                src_buf[u, at2, TILE:] = h2
            out_t = lax.dot_general(col_w[sj], tgt_buf[u], (((1,), (1,)), ((), ())),
                                    preferred_element_type=jnp.float32)
            out_s = lax.dot_general(row_w[ti], src_buf[u], (((1,), (0,)), ((), ())),
                                    preferred_element_type=jnp.float32)
            row_acc[ti] += alive * out_t
            col_acc[sj] += react * out_s
        return 0

    lax.fori_loop(0, (count[0] + (UNROLL - 1)) // UNROLL, visit, 0)

    def finish(block, acc, out, sign):
        x = [block[:, k, :] for k in range(3)]
        a = [block[:, 3 + k, :] for k in range(3)]
        qs = [acc[:, k, 0:TILE] + acc[:, 6 + k, 0:TILE] for k in range(6)]
        fs = [acc[:, k, TILE:] + acc[:, 6 + k, TILE:] for k in range(6)]
        for k in range(3):
            m, n = (k + 1) % 3, (k + 2) % 3
            velocity = x[m] * qs[n] - x[n] * qs[m] - qs[3 + k]
            steep = x[m] * fs[n] - x[n] * fs[m] - fs[3 + k]
            turn = a[m] * qs[n] - a[n] * qs[m]
            out[:, k, :] = biot_factor * velocity
            out[:, 3 + k, :] = biot_factor * (turn - (3.0 * sign) * steep)
            if k < 2:
                out[:, 6 + k, :] = jnp.zeros_like(velocity)

    finish(row_blk, row_acc, row_out, 1.0)
    finish(col_blk, col_acc, col_out, -1.0)


def scatter_kernel(nrows, ncols, tiles, row_terms, col_terms, counts, vel, stretch, held, send, recv):
    barrier = greet(nrows, ncols)
    row = lax.axis_index("row")
    col = lax.axis_index("col")
    pl.semaphore_wait(barrier, nrows + ncols - 2)
    copies = []
    for n, (axis, k) in enumerate(peers(nrows, ncols)):
        size, me = (ncols, col) if axis == "col" else (nrows, row)
        terms = row_terms if axis == "col" else col_terms
        other = lax.rem(me + k, size)
        copy = pltpu.make_async_remote_copy(
            src_ref=terms.at[other],
            dst_ref=held.at[n],
            send_sem=send.at[n],
            recv_sem=recv.at[n],
            device_id={axis: other},
            device_id_type=MESH,
        )
        copy.start()
        copies.append(copy)
    total = row_terms[col] + col_terms[row]
    for n, copy in enumerate(copies):
        copy.wait_recv()
        total = total + held[n]
    lane = lax.broadcasted_iota(jnp.int32, (8, TILE), 1)
    for t in range(tiles):
        part = slice(t * TILE, (t + 1) * TILE)
        value = jnp.where(lane < counts[t], total[t], 0.0)
        vel[:, part] = value[0:3]
        stretch[:, part] = value[3:6]
    for copy in copies:
        copy.wait_send()


def shards(nrows, ncols, positions, strengths, cores, order, tile_counts, pair_slots, pair_count):
    tiles = tile_counts.shape[0]
    others = nrows + ncols - 2
    f32 = jnp.float32
    row_blk, col_blk = pl.pallas_call(
        functools.partial(gather_kernel, nrows, ncols, tiles),
        out_shape=(
            jax.ShapeDtypeStruct((ncols, tiles, 8, TILE), f32),
            jax.ShapeDtypeStruct((nrows, tiles, 8, TILE), f32),
        ),
        in_specs=[VMEM, VMEM, VMEM, VMEM, SMEM],
        out_specs=(VMEM, VMEM),
        scratch_shapes=[
            pltpu.VMEM((tiles, 8, TILE), f32),
            pltpu.VMEM((tiles, 8, TILE), f32),
            pltpu.SemaphoreType.DMA((others,)),
            pltpu.SemaphoreType.DMA((others,)),
        ],
        compiler_params=pltpu.CompilerParams(collective_id=0, has_side_effects=True),
        name="gather_tiles",
    )(positions, strengths, cores.reshape(tiles, TILE), order.reshape(tiles, TILE), tile_counts)
    nt, ns = ncols * tiles, nrows * tiles
    row_terms, col_terms = pl.pallas_call(
        functools.partial(pair_kernel, nrows, ncols, tiles),
        out_shape=(
            jax.ShapeDtypeStruct((nt, 8, TILE), f32),
            jax.ShapeDtypeStruct((ns, 8, TILE), f32),
        ),
        in_specs=[SMEM, SMEM, VMEM, VMEM],
        out_specs=(VMEM, VMEM),
        scratch_shapes=[
            pltpu.VMEM((nt, TILE, 8), f32),
            pltpu.VMEM((nt, 16, 2 * TILE), jnp.bfloat16),
            pltpu.VMEM((ns, 16, 2 * TILE), jnp.bfloat16),
            pltpu.VMEM((nt, 16, 2 * TILE), f32),
            pltpu.VMEM((ns, 16, 2 * TILE), f32),
            pltpu.VMEM((UNROLL, 2 * TILE, 2 * TILE), jnp.bfloat16),
            pltpu.VMEM((UNROLL, 2 * TILE, 2 * TILE), jnp.bfloat16),
        ],
        compiler_params=pltpu.CompilerParams(vmem_limit_bytes=32 * 1024 * 1024),
        name="pair_terms",
    )(pair_slots, pair_count, row_blk.reshape(nt, 8, TILE), col_blk.reshape(ns, 8, TILE))
    return pl.pallas_call(
        functools.partial(scatter_kernel, nrows, ncols, tiles),
        out_shape=(
            jax.ShapeDtypeStruct((3, tiles * TILE), f32),
            jax.ShapeDtypeStruct((3, tiles * TILE), f32),
        ),
        in_specs=[VMEM, VMEM, SMEM],
        out_specs=(VMEM, VMEM),
        scratch_shapes=[
            pltpu.VMEM((others, tiles, 8, TILE), f32),
            pltpu.SemaphoreType.DMA((others,)),
            pltpu.SemaphoreType.DMA((others,)),
        ],
        compiler_params=pltpu.CompilerParams(collective_id=1, has_side_effects=True),
        name="sum_terms",
    )(row_terms.reshape(ncols, tiles, 8, TILE), col_terms.reshape(nrows, tiles, 8, TILE), tile_counts)


def solution(mesh):
    whole = ("groups", "row", "col")
    in_specs = (P(None, whole), P(None, whole), P(whole), P(whole), P(whole), P(None, whole), P(whole))
    out_specs = (P(None, whole), P(None, whole))
    body = functools.partial(shards, mesh.shape["row"], mesh.shape["col"])
    return jax.shard_map(body, mesh=mesh, in_specs=in_specs, out_specs=out_specs, check_vma=False)
```

```python
import functools
import math

import jax
import jax.numpy as jnp
from jax import lax
from jax.experimental import pallas as pl
from jax.experimental.pallas import tpu as pltpu
from jax.sharding import PartitionSpec as P

TILE = 128
MESH = pl.DeviceIdType.MESH
VMEM = pl.BlockSpec(memory_space=pltpu.VMEM)
SMEM = pl.BlockSpec(memory_space=pltpu.SMEM)
UNROLL = 4
CHUNK = 16

biot_factor = -1.0 / (4.0 * math.pi)


def peers(nrows, ncols):
    return [("col", k) for k in range(1, ncols)] + [("row", k) for k in range(1, nrows)]


def greet(nrows, ncols):
    barrier = pltpu.get_barrier_semaphore()
    for axis, k in peers(nrows, ncols):
        size = ncols if axis == "col" else nrows
        other = lax.rem(lax.axis_index(axis) + k, size)
        pl.semaphore_signal(barrier, inc=1, device_id={axis: other}, device_id_type=MESH)
    return barrier


def split(value):
    high = value.astype(jnp.bfloat16)
    return high, (value - high.astype(jnp.float32)).astype(jnp.bfloat16)


def cross(left, right):
    return [left[(k + 1) % 3] * right[(k + 2) % 3] - left[(k + 2) % 3] * right[(k + 1) % 3] for k in range(3)]


def wake_kernel(nrows, ncols, tiles, slots, count, counts, slot_rows, pos, strg, cores, order,
                vel, stretch, raw, row_blk, col_blk, across, stage, row_w, col_w, tgt_buf, src_buf,
                tgt_terms, src_terms, row_sum, col_sum, row_held, col_held, send, recv):
    barrier = greet(nrows, ncols)
    row = lax.axis_index("row")
    col = lax.axis_index("col")
    num_slots = slot_rows.shape[1]
    lane = lax.broadcasted_iota(jnp.int32, (8, TILE), 1)
    sub = lax.broadcasted_iota(jnp.int32, (8, TILE), 0)
    own_row = pl.multiple_of(col * tiles, tiles)
    own_col = pl.multiple_of(row * tiles, tiles)

    for t in range(tiles):
        part = slice(t * TILE, (t + 1) * TILE)
        raw[t, 0:3, :] = pos[:, part]
        raw[t, 3:6, :] = strg[:, part]
        raw[t, 6:7, :] = cores[t : t + 1, :]
        raw[t, 7:8, :] = cores[t : t + 1, :]
    for t in range(tiles):
        spot = jnp.broadcast_to(order[t : t + 1, :], (8, TILE))
        inner = spot % TILE
        outer = spot // TILE
        found = jnp.zeros((8, TILE), jnp.float32)
        for s in range(tiles):
            found = jnp.where(outer == s, jnp.take_along_axis(raw[s], inner, axis=1), found)
        keep = (lane < counts[t]) | (sub < 3) | (sub > 5)
        found = jnp.where(keep, found, 0.0)
        row_blk[own_row + t] = found
        col_blk[own_col + t] = found

    pl.semaphore_wait(barrier, nrows + ncols - 2)
    copies = []
    for n, (axis, k) in enumerate(peers(nrows, ncols)):
        size, me, block, at = (ncols, col, row_blk, own_row) if axis == "col" else (nrows, row, col_blk, own_col)
        copy = pltpu.make_async_remote_copy(
            src_ref=block.at[pl.ds(at, tiles)],
            dst_ref=block.at[pl.ds(at, tiles)],
            send_sem=send.at[0, n],
            recv_sem=recv.at[0, n],
            device_id={axis: lax.rem(me + k, size)},
            device_id_type=MESH,
        )
        copy.start()
        copies.append(copy)

    stage[...] = jnp.zeros_like(stage)

    def weights(block, at, out):
        some = block.at[pl.ds(at, tiles)]
        x = [some[:, k, :] for k in range(3)]
        a = [some[:, 3 + k, :] for k in range(3)]
        for k, value in enumerate(a + cross(x, a)):
            high = value.astype(jnp.bfloat16).astype(jnp.float32)
            stage[:, k, :] = high
            stage[:, 6 + k, :] = value - high
        for t in range(tiles):
            both = stage[t].astype(jnp.bfloat16)
            out[at + t, :, 0:TILE] = both
            out[at + t, :, TILE:] = both

    def prepare_row(k):
        at = pl.multiple_of(lax.rem(col + k, ncols) * tiles, tiles)
        weights(row_blk, at, row_w)
        for t in range(tiles):
            across[at + t] = row_blk[at + t].T

    def prepare_col(k):
        weights(col_blk, pl.multiple_of(lax.rem(row + k, nrows) * tiles, tiles), col_w)

    def pair(u, s, ti, sj, react):
        src = col_blk[sj]
        xj = [src[k : k + 1, :] for k in range(7)]
        hj = 0.5 * xj[6] * xj[6]
        for c in range(TILE // CHUNK):
            at = slice(c * CHUNK, (c + 1) * CHUNK)
            at2 = slice(TILE + c * CHUNK, TILE + (c + 1) * CHUNK)
            tgt = across[ti, at, :]
            xi = [tgt[:, k : k + 1] for k in range(7)]
            hi = 0.5 * xi[6] * xi[6]
            dx = xi[0] - xj[0]
            dy = xi[1] - xj[1]
            dz = xi[2] - xj[2]
            s2 = hi + hj
            d = dx * dx + dy * dy + dz * dz + s2
            inv = lax.rsqrt(d)
            inv2 = inv * inv
            inv3 = inv2 * inv
            w = s2 * (inv3 * inv2)
            q = inv3 + 1.5 * w
            f = (q + w) * inv2
            g = f * (xi[3] * dx + xi[4] * dy + xi[5] * dz)
            q1, q2 = split(q)
            g1, g2 = split(g)
            tgt_buf[u, at, 0:TILE] = q1
            tgt_buf[u, at, TILE:] = q2
            tgt_buf[u, at2, 0:TILE] = g1
            tgt_buf[u, at2, TILE:] = g2
            if react:
                h = f * (xj[3] * dx + xj[4] * dy + xj[5] * dz)
                h1, h2 = split(h)
                src_buf[u, at, 0:TILE] = q1
                src_buf[u, at, TILE:] = h1
                src_buf[u, at2, 0:TILE] = q2
                src_buf[u, at2, TILE:] = h2
        out = lax.dot_general(col_w[sj], tgt_buf[u], (((1,), (1,)), ((), ())), preferred_element_type=jnp.float32)
        tgt_terms[s, 0:6, :] = out[0:6] + out[6:12]
        if react:
            out = lax.dot_general(row_w[ti], src_buf[u], (((1,), (0,)), ((), ())), preferred_element_type=jnp.float32)
            src_terms[s, 0:6, :] = out[0:6] + out[6:12]

    prepare_row(0)
    prepare_col(0)
    src_terms[0:tiles] = jnp.zeros((tiles, 8, 2 * TILE), jnp.float32)

    def diagonal(step, _):
        for u in range(2):
            t = step * 2 + u
            pair(u, t, own_row + t, own_col + t, False)
        return 0

    lax.fori_loop(0, tiles // 2, diagonal, 0)
    for copy in copies:
        copy.wait_recv()
    for k in range(1, ncols):
        prepare_row(k)
    for k in range(1, nrows):
        prepare_col(k)

    def visit(step, _):
        for u in range(UNROLL):
            s = tiles + step * UNROLL + u
            pair(u, s, slots[0, s], slots[1, s], True)
        return 0

    lax.fori_loop(0, (num_slots - tiles) // UNROLL, visit, 0)

    first = slot_rows[0:1, :]
    second = slot_rows[1:2, :]
    slot = lax.broadcasted_iota(jnp.int32, (1, num_slots), 1)
    first = jnp.where(slot < tiles, own_row + slot, first)
    gi = row * (ncols * tiles) + first
    gj = ((second // tiles) * ncols + col) * tiles + second % tiles
    alive = slot < count[0]
    row_sel = jnp.where(alive, first, -1)
    col_sel = jnp.where(alive & (gi != gj) & (slot >= tiles), second, -1)

    def finish(select, terms, block, out, sign):
        size = block.shape[0]
        here = lax.broadcasted_iota(jnp.int32, (size, num_slots), 0)
        hot = jnp.where(here == select, 1.0, 0.0).astype(jnp.bfloat16)
        qs, fs = [], []
        for k in range(6):
            high, low = split(terms[:, k, :])
            value = jnp.dot(hot, high, preferred_element_type=jnp.float32)
            value += jnp.dot(hot, low, preferred_element_type=jnp.float32)
            qs.append(value[:, 0:TILE])
            fs.append(value[:, TILE:])
        x = [block[:, k, :] for k in range(3)]
        a = [block[:, 3 + k, :] for k in range(3)]
        velocity = cross(x, qs[0:3])
        turn = cross(a, qs[0:3])
        steep = cross(x, fs[0:3])
        for k in range(3):
            v = biot_factor * (velocity[k] - qs[3 + k])
            w = biot_factor * (turn[k] - (3.0 * sign) * (steep[k] - fs[3 + k]))
            out[:, k] = v.reshape(size // tiles, tiles, TILE)
            out[:, 3 + k] = w.reshape(size // tiles, tiles, TILE)

    for copy in copies:
        copy.wait_send()

    def send_all(axis, first_sem, size, me, sums, held):
        started = []
        for k in range(1, size):
            other = lax.rem(me + k, size)
            copy = pltpu.make_async_remote_copy(
                src_ref=sums.at[other],
                dst_ref=held.at[k - 1],
                send_sem=send.at[1, first_sem + k - 1],
                recv_sem=recv.at[1, first_sem + k - 1],
                device_id={axis: other},
                device_id_type=MESH,
            )
            copy.start()
            started.append((copy, held.at[k - 1]))
        return started

    finish(row_sel, tgt_terms, row_blk, row_sum, 1.0)
    started = send_all("col", 0, ncols, col, row_sum, row_held)
    finish(col_sel, src_terms, col_blk, col_sum, -1.0)
    started += send_all("row", ncols - 1, nrows, row, col_sum, col_held)
    total = row_sum[col] + col_sum[row]
    for copy, held in started:
        copy.wait_recv()
        total = total + held[...]
    for t in range(tiles):
        part = slice(t * TILE, (t + 1) * TILE)
        live = lane[0:1, :] < counts[t]
        for k in range(3):
            vel[k : k + 1, part] = jnp.where(live, total[k, t : t + 1, :], 0.0)
            stretch[k : k + 1, part] = jnp.where(live, total[3 + k, t : t + 1, :], 0.0)
    for copy, _ in started:
        copy.wait_send()


def shards(nrows, ncols, positions, strengths, cores, order, tile_counts, pair_slots, pair_count):
    tiles = tile_counts.shape[0]
    num_slots = pair_slots.shape[1]
    others = nrows + ncols - 2
    nt, ns = ncols * tiles, nrows * tiles
    f32, bf16 = jnp.float32, jnp.bfloat16
    return pl.pallas_call(
        functools.partial(wake_kernel, nrows, ncols, tiles),
        out_shape=(
            jax.ShapeDtypeStruct((3, tiles * TILE), f32),
            jax.ShapeDtypeStruct((3, tiles * TILE), f32),
        ),
        in_specs=[SMEM, SMEM, SMEM, VMEM, VMEM, VMEM, VMEM, VMEM],
        out_specs=(VMEM, VMEM),
        scratch_shapes=[
            pltpu.VMEM((tiles, 8, TILE), f32),
            pltpu.VMEM((nt, 8, TILE), f32),
            pltpu.VMEM((ns, 8, TILE), f32),
            pltpu.VMEM((nt, TILE, 8), f32),
            pltpu.VMEM((tiles, 16, TILE), f32),
            pltpu.VMEM((nt, 16, 2 * TILE), bf16),
            pltpu.VMEM((ns, 16, 2 * TILE), bf16),
            pltpu.VMEM((UNROLL, 2 * TILE, 2 * TILE), bf16),
            pltpu.VMEM((UNROLL, 2 * TILE, 2 * TILE), bf16),
            pltpu.VMEM((num_slots, 8, 2 * TILE), f32),
            pltpu.VMEM((num_slots, 8, 2 * TILE), f32),
            pltpu.VMEM((ncols, 6, tiles, TILE), f32),
            pltpu.VMEM((nrows, 6, tiles, TILE), f32),
            pltpu.VMEM((ncols - 1, 6, tiles, TILE), f32),
            pltpu.VMEM((nrows - 1, 6, tiles, TILE), f32),
            pltpu.SemaphoreType.DMA((2, others)),
            pltpu.SemaphoreType.DMA((2, others)),
        ],
        compiler_params=pltpu.CompilerParams(
            collective_id=0, has_side_effects=True, vmem_limit_bytes=32 * 1024 * 1024
        ),
        name="wake",
    )(pair_slots, pair_count, tile_counts, pair_slots, positions, strengths,
      cores.reshape(tiles, TILE), order.reshape(tiles, TILE))


def solution(mesh):
    whole = ("groups", "row", "col")
    in_specs = (P(None, whole), P(None, whole), P(whole), P(whole), P(whole), P(None, whole), P(whole))
    out_specs = (P(None, whole), P(None, whole))
    body = functools.partial(shards, mesh.shape["row"], mesh.shape["col"])
    return jax.shard_map(body, mesh=mesh, in_specs=in_specs, out_specs=out_specs, check_vma=False)
```

```python
import functools
import math

import jax
import jax.numpy as jnp
from jax import lax
from jax.experimental import pallas as pl
from jax.experimental.pallas import tpu as pltpu
from jax.sharding import PartitionSpec as P

TILE = 128
MESH = pl.DeviceIdType.MESH
VMEM = pl.BlockSpec(memory_space=pltpu.VMEM)
SMEM = pl.BlockSpec(memory_space=pltpu.SMEM)
HBM = pl.BlockSpec(memory_space=pltpu.HBM)
UNROLL = 8
CHUNK = 16

biot_factor = -1.0 / (4.0 * math.pi)


def peers(nrows, ncols):
    return [("col", k) for k in range(1, ncols)] + [("row", k) for k in range(1, nrows)]


def greet(nrows, ncols):
    barrier = pltpu.get_barrier_semaphore()
    for axis, k in peers(nrows, ncols):
        size = ncols if axis == "col" else nrows
        other = lax.rem(lax.axis_index(axis) + k, size)
        pl.semaphore_signal(barrier, inc=1, device_id={axis: other}, device_id_type=MESH)
    return barrier


def split(value):
    high = value.astype(jnp.bfloat16)
    return high, (value - high.astype(jnp.float32)).astype(jnp.bfloat16)


def cross(left, right):
    return [left[(k + 1) % 3] * right[(k + 2) % 3] - left[(k + 2) % 3] * right[(k + 1) % 3] for k in range(3)]


def wake_kernel(nrows, ncols, tiles, slots, count, counts, slot_rows_in, pos_in, strg_in, cores_in, order_in,
                vel, stretch, slot_rows, pos, strg, cores, order, raw, row_blk, col_blk, spread, ones, stage, row_w, col_w, tgt_buf, src_buf,
                tgt_terms, src_terms, row_sum, col_sum, row_held, col_held, load, send, recv):
    pairs_in = [(pos_in, pos), (strg_in, strg), (cores_in, cores), (order_in, order), (slot_rows_in, slot_rows)]
    loads = [pltpu.make_async_copy(src, dst, load.at[n]) for n, (src, dst) in enumerate(pairs_in)]
    for copy in loads:
        copy.start()
    barrier = greet(nrows, ncols)
    row = lax.axis_index("row")
    col = lax.axis_index("col")
    num_slots = slot_rows.shape[1]
    lane = lax.broadcasted_iota(jnp.int32, (8, TILE), 1)
    sub = lax.broadcasted_iota(jnp.int32, (8, TILE), 0)
    own_row = pl.multiple_of(col * tiles, tiles)
    own_col = pl.multiple_of(row * tiles, tiles)

    stage[...] = jnp.zeros_like(stage)
    rank = lax.broadcasted_iota(jnp.int32, (16, TILE), 0)
    for k in range(3):
        ones[:, k * TILE : (k + 1) * TILE] = jnp.where((rank == k) | (rank == 6 + k), 1.0, 0.0).astype(jnp.bfloat16)
    ones[:, 3 * TILE :] = jnp.where((rank > 11) & (rank < 15), 1.0, 0.0).astype(jnp.bfloat16)
    for copy in loads:
        copy.wait()
    for t in range(tiles):
        part = slice(t * TILE, (t + 1) * TILE)
        raw[t, 0:3, :] = pos[:, part]
        raw[t, 3:6, :] = strg[:, part]
        raw[t, 6:7, :] = cores[t : t + 1, :]
        raw[t, 7:8, :] = cores[t : t + 1, :]
    for t in range(tiles):
        spot = jnp.broadcast_to(order[t : t + 1, :], (8, TILE))
        inner = spot % TILE
        outer = spot // TILE
        found = jnp.zeros((8, TILE), jnp.float32)
        for s in range(tiles):
            found = jnp.where(outer == s, jnp.take_along_axis(raw[s], inner, axis=1), found)
        keep = (lane < counts[t]) | (sub < 3) | (sub > 5)
        found = jnp.where(keep, found, 0.0)
        row_blk[own_row + t] = found
        col_blk[own_col + t] = found

    pl.semaphore_wait(barrier, nrows + ncols - 2)
    copies = []
    for n, (axis, k) in enumerate(peers(nrows, ncols)):
        size, me, block, at = (ncols, col, row_blk, own_row) if axis == "col" else (nrows, row, col_blk, own_col)
        copy = pltpu.make_async_remote_copy(
            src_ref=block.at[pl.ds(at, tiles)],
            dst_ref=block.at[pl.ds(at, tiles)],
            send_sem=send.at[0, n],
            recv_sem=recv.at[0, n],
            device_id={axis: lax.rem(me + k, size)},
            device_id_type=MESH,
        )
        copy.start()
        copies.append(copy)

    def weights(block, at, out):
        some = block.at[pl.ds(at, tiles)]
        x = [some[:, k, :] for k in range(3)]
        a = [some[:, 3 + k, :] for k in range(3)]
        for k, value in enumerate(a + cross(x, a)):
            high = value.astype(jnp.bfloat16).astype(jnp.float32)
            stage[:, k, :] = high
            stage[:, 6 + k, :] = value - high
        sigma = some[:, 6, :]
        rest = 0.5 * sigma * sigma
        for k in range(3):
            high = rest.astype(jnp.bfloat16).astype(jnp.float32)
            stage[:, 12 + k, :] = high
            rest = rest - high
        for t in range(tiles):
            both = stage[t].astype(jnp.bfloat16)
            out[at + t, :, 0:TILE] = both
            out[at + t, :, TILE:] = both

    def prepare_row(k):
        at = pl.multiple_of(lax.rem(col + k, ncols) * tiles, tiles)
        weights(row_blk, at, row_w)
        for t in range(tiles):
            column = row_blk[at + t].T
            for j in range(3):
                spread[at + t, j] = jnp.broadcast_to(column[:, j : j + 1], (TILE, TILE))
            rest = lax.dot_general(row_w[at + t, :, 0:TILE], ones[...], (((0,), (0,)), ((), ())),
                                   preferred_element_type=jnp.float32)
            for j in range(4):
                spread[at + t, 3 + j] = rest[:, j * TILE : (j + 1) * TILE]

    def prepare_col(k):
        weights(col_blk, pl.multiple_of(lax.rem(row + k, nrows) * tiles, tiles), col_w)

    def pair(u, s, ti, sj, react):
        src = col_blk[sj]
        xj = [src[k : k + 1, :] for k in range(7)]
        hj = 0.5 * xj[6] * xj[6]
        for c in range(TILE // CHUNK):
            at = slice(c * CHUNK, (c + 1) * CHUNK)
            at2 = slice(TILE + c * CHUNK, TILE + (c + 1) * CHUNK)
            xi = [spread[ti, k, at, :] for k in range(7)]
            dx = xi[0] - xj[0]
            dy = xi[1] - xj[1]
            dz = xi[2] - xj[2]
            s2 = xi[6] + hj
            d = dx * dx + dy * dy + dz * dz + s2
            inv = lax.rsqrt(d)
            inv2 = inv * inv
            inv3 = inv2 * inv
            w = s2 * (inv3 * inv2)
            q = inv3 + 1.5 * w
            f = (q + w) * inv2
            g = f * (xi[3] * dx + xi[4] * dy + xi[5] * dz)
            q1, q2 = split(q)
            g1, g2 = split(g)
            tgt_buf[u, at, 0:TILE] = q1
            tgt_buf[u, at, TILE:] = q2
            tgt_buf[u, at2, 0:TILE] = g1
            tgt_buf[u, at2, TILE:] = g2
            if react:
                h = f * (xj[3] * dx + xj[4] * dy + xj[5] * dz)
                h1, h2 = split(h)
                src_buf[u, at, 0:TILE] = q1
                src_buf[u, at, TILE:] = h1
                src_buf[u, at2, 0:TILE] = q2
                src_buf[u, at2, TILE:] = h2
        out = lax.dot_general(col_w[sj], tgt_buf[u], (((1,), (1,)), ((), ())), preferred_element_type=jnp.float32)
        tgt_terms[s, 0:6, :] = out[0:6] + out[6:12]
        if react:
            out = lax.dot_general(row_w[ti], src_buf[u], (((1,), (0,)), ((), ())), preferred_element_type=jnp.float32)
            src_terms[s, 0:6, :] = out[0:6] + out[6:12]

    prepare_row(0)
    prepare_col(0)
    src_terms[0:tiles] = jnp.zeros((tiles, 8, 2 * TILE), jnp.float32)

    def diagonal(step, _):
        for u in range(4):
            t = step * 4 + u
            pair(u, t, own_row + t, own_col + t, False)
        return 0

    lax.fori_loop(0, tiles // 4, diagonal, 0)
    for copy in copies:
        copy.wait_recv()
    lax.fori_loop(1, ncols, lambda k, _: (prepare_row(k), 0)[1], 0)
    lax.fori_loop(1, nrows, lambda k, _: (prepare_col(k), 0)[1], 0)

    def visit(step, _):
        for u in range(UNROLL):
            s = tiles + step * UNROLL + u
            pair(u, s, slots[0, s], slots[1, s], True)
        return 0

    lax.fori_loop(0, (num_slots - tiles) // UNROLL, visit, 0)

    first = slot_rows[0:1, :]
    second = slot_rows[1:2, :]
    slot = lax.broadcasted_iota(jnp.int32, (1, num_slots), 1)
    first = jnp.where(slot < tiles, own_row + slot, first)
    gi = row * (ncols * tiles) + first
    gj = ((second // tiles) * ncols + col) * tiles + second % tiles
    alive = slot < count[0]
    row_sel = jnp.where(alive, first, -1)
    col_sel = jnp.where(alive & (gi != gj) & (slot >= tiles), second, -1)

    def finish(select, terms, block, out, sign):
        size = block.shape[0]
        here = lax.broadcasted_iota(jnp.int32, (size, num_slots), 0)
        hot = jnp.where(here == select, 1.0, 0.0).astype(jnp.bfloat16)
        qs, fs = [], []
        for k in range(6):
            high, low = split(terms[:, k, :])
            value = jnp.dot(hot, high, preferred_element_type=jnp.float32)
            value += jnp.dot(hot, low, preferred_element_type=jnp.float32)
            qs.append(value[:, 0:TILE])
            fs.append(value[:, TILE:])
        x = [block[:, k, :] for k in range(3)]
        a = [block[:, 3 + k, :] for k in range(3)]
        velocity = cross(x, qs[0:3])
        turn = cross(a, qs[0:3])
        steep = cross(x, fs[0:3])
        for k in range(3):
            v = biot_factor * (velocity[k] - qs[3 + k])
            w = biot_factor * (turn[k] - (3.0 * sign) * (steep[k] - fs[3 + k]))
            out[:, k] = v.reshape(size // tiles, tiles, TILE)
            out[:, 3 + k] = w.reshape(size // tiles, tiles, TILE)

    for copy in copies:
        copy.wait_send()

    def send_all(axis, first_sem, size, me, sums, held):
        started = []
        for k in range(1, size):
            other = lax.rem(me + k, size)
            copy = pltpu.make_async_remote_copy(
                src_ref=sums.at[other],
                dst_ref=held.at[k - 1],
                send_sem=send.at[1, first_sem + k - 1],
                recv_sem=recv.at[1, first_sem + k - 1],
                device_id={axis: other},
                device_id_type=MESH,
            )
            copy.start()
            started.append((copy, held.at[k - 1]))
        return started

    finish(row_sel, tgt_terms, row_blk, row_sum, 1.0)
    started = send_all("col", 0, ncols, col, row_sum, row_held)
    finish(col_sel, src_terms, col_blk, col_sum, -1.0)
    started += send_all("row", ncols - 1, nrows, row, col_sum, col_held)
    total = row_sum[col] + col_sum[row]
    for copy, held in started:
        copy.wait_recv()
        total = total + held[...]
    for t in range(tiles):
        part = slice(t * TILE, (t + 1) * TILE)
        live = lane[0:1, :] < counts[t]
        for k in range(3):
            vel[k : k + 1, part] = jnp.where(live, total[k, t : t + 1, :], 0.0)
            stretch[k : k + 1, part] = jnp.where(live, total[3 + k, t : t + 1, :], 0.0)
    for copy, _ in started:
        copy.wait_send()


def shards(nrows, ncols, positions, strengths, cores, order, tile_counts, pair_slots, pair_count):
    tiles = tile_counts.shape[0]
    num_slots = pair_slots.shape[1]
    others = nrows + ncols - 2
    nt, ns = ncols * tiles, nrows * tiles
    f32, bf16 = jnp.float32, jnp.bfloat16
    return pl.pallas_call(
        functools.partial(wake_kernel, nrows, ncols, tiles),
        out_shape=(
            jax.ShapeDtypeStruct((3, tiles * TILE), f32),
            jax.ShapeDtypeStruct((3, tiles * TILE), f32),
        ),
        in_specs=[SMEM, SMEM, SMEM, HBM, HBM, HBM, HBM, HBM],
        out_specs=(VMEM, VMEM),
        scratch_shapes=[
            pltpu.VMEM((2, num_slots), jnp.int32),
            pltpu.VMEM((3, tiles * TILE), f32),
            pltpu.VMEM((3, tiles * TILE), f32),
            pltpu.VMEM((tiles, TILE), f32),
            pltpu.VMEM((tiles, TILE), jnp.int32),
            pltpu.VMEM((tiles, 8, TILE), f32),
            pltpu.VMEM((nt, 8, TILE), f32),
            pltpu.VMEM((ns, 8, TILE), f32),
            pltpu.VMEM((nt, 7, TILE, TILE), f32),
            pltpu.VMEM((16, 4 * TILE), bf16),
            pltpu.VMEM((tiles, 16, TILE), f32),
            pltpu.VMEM((nt, 16, 2 * TILE), bf16),
            pltpu.VMEM((ns, 16, 2 * TILE), bf16),
            pltpu.VMEM((UNROLL, 2 * TILE, 2 * TILE), bf16),
            pltpu.VMEM((UNROLL, 2 * TILE, 2 * TILE), bf16),
            pltpu.VMEM((num_slots, 8, 2 * TILE), f32),
            pltpu.VMEM((num_slots, 8, 2 * TILE), f32),
            pltpu.VMEM((ncols, 6, tiles, TILE), f32),
            pltpu.VMEM((nrows, 6, tiles, TILE), f32),
            pltpu.VMEM((ncols - 1, 6, tiles, TILE), f32),
            pltpu.VMEM((nrows - 1, 6, tiles, TILE), f32),
            pltpu.SemaphoreType.DMA((5,)),
            pltpu.SemaphoreType.DMA((2, others)),
            pltpu.SemaphoreType.DMA((2, others)),
        ],
        compiler_params=pltpu.CompilerParams(
            collective_id=0, has_side_effects=True, vmem_limit_bytes=56 * 1024 * 1024
        ),
        name="wake",
    )(pair_slots, pair_count, tile_counts, pair_slots, positions, strengths,
      cores.reshape(tiles, TILE), order.reshape(tiles, TILE))


def solution(mesh):
    whole = ("groups", "row", "col")
    in_specs = (P(None, whole), P(None, whole), P(whole), P(whole), P(whole), P(None, whole), P(whole))
    out_specs = (P(None, whole), P(None, whole))
    body = functools.partial(shards, mesh.shape["row"], mesh.shape["col"])
    return jax.shard_map(body, mesh=mesh, in_specs=in_specs, out_specs=out_specs, check_vma=False)
```

```python
import functools
import math

import jax
import jax.numpy as jnp
from jax import lax
from jax.experimental import pallas as pl
from jax.experimental.pallas import tpu as pltpu
from jax.sharding import PartitionSpec as P

TILE = 128
MESH = pl.DeviceIdType.MESH
VMEM = pl.BlockSpec(memory_space=pltpu.VMEM)
SMEM = pl.BlockSpec(memory_space=pltpu.SMEM)
HBM = pl.BlockSpec(memory_space=pltpu.HBM)
UNROLL = 14
CHUNK = 16

biot_factor = -1.0 / (4.0 * math.pi)


def peers(nrows, ncols):
    return [("col", k) for k in range(1, ncols)] + [("row", k) for k in range(1, nrows)]


def greet(nrows, ncols):
    barrier = pltpu.get_barrier_semaphore()
    for axis, k in peers(nrows, ncols):
        size = ncols if axis == "col" else nrows
        other = lax.rem(lax.axis_index(axis) + k, size)
        pl.semaphore_signal(barrier, inc=1, device_id={axis: other}, device_id_type=MESH)
    return barrier


def split(value):
    high = value.astype(jnp.bfloat16)
    return high, (value - high.astype(jnp.float32)).astype(jnp.bfloat16)


def cross(left, right):
    return [left[(k + 1) % 3] * right[(k + 2) % 3] - left[(k + 2) % 3] * right[(k + 1) % 3] for k in range(3)]


def wake_kernel(nrows, ncols, tiles, slots, count, counts, slot_rows_in, pos_in, strg_in, cores_in, order_in,
                sums_out, slot_rows, pos, strg, cores, order, raw, row_blk, col_blk, spread, ones, stage, row_w, col_w, tgt_buf, src_buf,
                tgt_terms, src_terms, row_sum, col_sum, row_held, col_held, load, send, recv):
    pairs_in = [(pos_in, pos), (strg_in, strg), (cores_in, cores), (order_in, order), (slot_rows_in, slot_rows)]
    loads = [pltpu.make_async_copy(src, dst, load.at[n]) for n, (src, dst) in enumerate(pairs_in)]
    for copy in loads:
        copy.start()
    barrier = greet(nrows, ncols)
    row = lax.axis_index("row")
    col = lax.axis_index("col")
    num_slots = slot_rows.shape[1]
    lane = lax.broadcasted_iota(jnp.int32, (8, TILE), 1)
    sub = lax.broadcasted_iota(jnp.int32, (8, TILE), 0)
    own_row = pl.multiple_of(col * tiles, tiles)
    own_col = pl.multiple_of(row * tiles, tiles)

    stage[...] = jnp.zeros_like(stage)
    rank = lax.broadcasted_iota(jnp.int32, (16, TILE), 0)
    for k in range(3):
        ones[:, k * TILE : (k + 1) * TILE] = jnp.where((rank == k) | (rank == 6 + k), 1.0, 0.0).astype(jnp.bfloat16)
    ones[:, 3 * TILE :] = jnp.where((rank > 11) & (rank < 15), 1.0, 0.0).astype(jnp.bfloat16)
    for copy in loads:
        copy.wait()
    for t in range(tiles):
        part = slice(t * TILE, (t + 1) * TILE)
        raw[t, 0:3, :] = pos[:, part]
        raw[t, 3:6, :] = strg[:, part]
        raw[t, 6:7, :] = cores[t : t + 1, :]
        raw[t, 7:8, :] = cores[t : t + 1, :]
    for t in range(tiles):
        spot = jnp.broadcast_to(order[t : t + 1, :], (8, TILE))
        inner = spot & (TILE - 1)
        outer = spot >> 7
        found = jnp.zeros((8, TILE), jnp.float32)
        for s in range(tiles):
            found = jnp.where(outer == s, jnp.take_along_axis(raw[s], inner, axis=1), found)
        keep = (lane < counts[t]) | (sub < 3) | (sub > 5)
        found = jnp.where(keep, found, 0.0)
        row_blk[own_row + t] = found
        col_blk[own_col + t] = found

    pl.semaphore_wait(barrier, nrows + ncols - 2)
    copies = []
    for n, (axis, k) in enumerate(peers(nrows, ncols)):
        size, me, block, at = (ncols, col, row_blk, own_row) if axis == "col" else (nrows, row, col_blk, own_col)
        copy = pltpu.make_async_remote_copy(
            src_ref=block.at[pl.ds(at, tiles)],
            dst_ref=block.at[pl.ds(at, tiles)],
            send_sem=send.at[0, n],
            recv_sem=recv.at[0, n],
            device_id={axis: lax.rem(me + k, size)},
            device_id_type=MESH,
        )
        copy.start()
        copies.append(copy)

    def weights(block, at, out):
        some = block.at[pl.ds(at, tiles)]
        x = [some[:, k, :] for k in range(3)]
        a = [some[:, 3 + k, :] for k in range(3)]
        for k, value in enumerate(a + cross(x, a)):
            high = value.astype(jnp.bfloat16).astype(jnp.float32)
            stage[:, k, :] = high
            stage[:, 6 + k, :] = value - high
        sigma = some[:, 6, :]
        rest = 0.5 * sigma * sigma
        for k in range(3):
            high = rest.astype(jnp.bfloat16).astype(jnp.float32)
            stage[:, 12 + k, :] = high
            rest = rest - high
        for t in range(tiles):
            both = stage[t].astype(jnp.bfloat16)
            out[at + t, :, 0:TILE] = both
            out[at + t, :, TILE:] = both

    def prepare_row(k):
        at = pl.multiple_of(lax.rem(col + ncols - k, ncols) * tiles, tiles)
        weights(row_blk, at, row_w)
        for t in range(tiles):
            column = row_blk[at + t].T
            for j in range(3):
                spread[at + t, j] = jnp.broadcast_to(column[:, j : j + 1], (TILE, TILE))
            rest = lax.dot_general(row_w[at + t, :, 0:TILE], ones[...], (((0,), (0,)), ((), ())),
                                   preferred_element_type=jnp.float32)
            for j in range(4):
                spread[at + t, 3 + j] = rest[:, j * TILE : (j + 1) * TILE]

    def prepare_col(k):
        weights(col_blk, pl.multiple_of(lax.rem(row + nrows - k, nrows) * tiles, tiles), col_w)

    def pair(u, s, ti, sj, react):
        src = col_blk[sj]
        xj = [src[k : k + 1, :] for k in range(7)]
        hj = 0.5 * xj[6] * xj[6]
        for c in range(TILE // CHUNK):
            at = slice(c * CHUNK, (c + 1) * CHUNK)
            at2 = slice(TILE + c * CHUNK, TILE + (c + 1) * CHUNK)
            xi = [spread[ti, k, at, :] for k in range(7)]
            dx = xi[0] - xj[0]
            dy = xi[1] - xj[1]
            dz = xi[2] - xj[2]
            s2 = xi[6] + hj
            d = dx * dx + dy * dy + dz * dz + s2
            inv = lax.rsqrt(d)
            inv2 = inv * inv
            inv3 = inv2 * inv
            w = s2 * (inv3 * inv2)
            q = inv3 + 1.5 * w
            f = (q + w) * inv2
            g = f * (xi[3] * dx + xi[4] * dy + xi[5] * dz)
            q1, q2 = split(q)
            g1, g2 = split(g)
            tgt_buf[u, at, 0:TILE] = q1
            tgt_buf[u, at, TILE:] = q2
            tgt_buf[u, at2, 0:TILE] = g1
            tgt_buf[u, at2, TILE:] = g2
            if react:
                h = f * (xj[3] * dx + xj[4] * dy + xj[5] * dz)
                h1, h2 = split(h)
                src_buf[u, at, 0:TILE] = q1
                src_buf[u, at, TILE:] = h1
                src_buf[u, at2, 0:TILE] = q2
                src_buf[u, at2, TILE:] = h2
        out = lax.dot_general(col_w[sj], tgt_buf[u], (((1,), (1,)), ((), ())), preferred_element_type=jnp.float32)
        tgt_terms[s, 0:6, :] = out[0:6] + out[6:12]
        if react:
            out = lax.dot_general(row_w[ti], src_buf[u], (((1,), (0,)), ((), ())), preferred_element_type=jnp.float32)
            src_terms[s, 0:6, :] = out[0:6] + out[6:12]

    prepare_row(0)
    prepare_col(0)
    src_terms[0:tiles] = jnp.zeros((tiles, 8, 2 * TILE), jnp.float32)

    def diagonal(step, _):
        for u in range(4):
            t = step * 4 + u
            pair(u, t, own_row + t, own_col + t, False)
        return 0

    lax.fori_loop(0, tiles // 4, diagonal, 0)

    def arrived(axis, size, me, block, base, prepare):
        def step(k, _):
            other = lax.rem(me + size - k, size)
            place = block.at[pl.ds(pl.multiple_of(other * tiles, tiles), tiles)]
            pltpu.make_async_remote_copy(
                src_ref=place,
                dst_ref=place,
                send_sem=send.at[0, base + k - 1],
                recv_sem=recv.at[0, base + k - 1],
                device_id={axis: other},
                device_id_type=MESH,
            ).wait_recv()
            prepare(k)
            return 0

        lax.fori_loop(1, size, step, 0)

    arrived("col", ncols, col, row_blk, 0, prepare_row)
    arrived("row", nrows, row, col_blk, ncols - 1, prepare_col)

    def visit(step, _):
        for u in range(UNROLL):
            s = tiles + step * UNROLL + u
            pair(u, s, slots[0, s], slots[1, s], True)
        return 0

    lax.fori_loop(0, (num_slots - tiles) // UNROLL, visit, 0)

    first = slot_rows[0:1, :]
    second = slot_rows[1:2, :]
    slot = lax.broadcasted_iota(jnp.int32, (1, num_slots), 1)
    first = jnp.where(slot < tiles, own_row + slot, first)
    gi = row * (ncols * tiles) + first
    gj = ((second // tiles) * ncols + col) * tiles + second % tiles
    alive = slot < count[0]
    row_sel = jnp.where(alive, first, -1)
    col_sel = jnp.where(alive & (gi != gj) & (slot >= tiles), second, -1)

    def finish(select, terms, block, out, sign):
        size = block.shape[0]
        here = lax.broadcasted_iota(jnp.int32, (size, num_slots), 0)
        hot = jnp.where(here == select, 1.0, 0.0).astype(jnp.bfloat16)
        qs, fs = [], []
        for k in range(6):
            high, low = split(terms[:, k, :])
            value = jnp.dot(hot, high, preferred_element_type=jnp.float32)
            value += jnp.dot(hot, low, preferred_element_type=jnp.float32)
            qs.append(value[:, 0:TILE])
            fs.append(value[:, TILE:])
        x = [block[:, k, :] for k in range(3)]
        a = [block[:, 3 + k, :] for k in range(3)]
        velocity = cross(x, qs[0:3])
        turn = cross(a, qs[0:3])
        steep = cross(x, fs[0:3])
        for k in range(3):
            v = biot_factor * (velocity[k] - qs[3 + k])
            w = biot_factor * (turn[k] - (3.0 * sign) * (steep[k] - fs[3 + k]))
            out[:, k] = v.reshape(size // tiles, tiles, TILE)
            out[:, 3 + k] = w.reshape(size // tiles, tiles, TILE)

    for copy in copies:
        copy.wait_send()

    def send_all(axis, first_sem, size, me, sums, held):
        started = []
        for k in range(1, size):
            other = lax.rem(me + k, size)
            copy = pltpu.make_async_remote_copy(
                src_ref=sums.at[other],
                dst_ref=held.at[k - 1],
                send_sem=send.at[1, first_sem + k - 1],
                recv_sem=recv.at[1, first_sem + k - 1],
                device_id={axis: other},
                device_id_type=MESH,
            )
            copy.start()
            started.append((copy, held.at[k - 1]))
        return started

    finish(row_sel, tgt_terms, row_blk, row_sum, 1.0)
    started = send_all("col", 0, ncols, col, row_sum, row_held)
    finish(col_sel, src_terms, col_blk, col_sum, -1.0)
    started += send_all("row", ncols - 1, nrows, row, col_sum, col_held)
    total = row_sum[col] + col_sum[row]
    for copy, held in started:
        copy.wait_recv()
        total = total + held[...]
    for t in range(tiles):
        part = slice(t * TILE, (t + 1) * TILE)
        live = lane[0:1, :] < counts[t]
        for k in range(3):
            sums_out[k : k + 1, part] = jnp.where(live, total[k, t : t + 1, :], 0.0)
            sums_out[3 + k : 4 + k, part] = jnp.where(live, total[3 + k, t : t + 1, :], 0.0)
    for copy, _ in started:
        copy.wait_send()


def shards(nrows, ncols, positions, strengths, cores, order, tile_counts, pair_slots, pair_count):
    tiles = tile_counts.shape[0]
    num_slots = pair_slots.shape[1]
    others = nrows + ncols - 2
    nt, ns = ncols * tiles, nrows * tiles
    f32, bf16 = jnp.float32, jnp.bfloat16
    sums = pl.pallas_call(
        functools.partial(wake_kernel, nrows, ncols, tiles),
        out_shape=jax.ShapeDtypeStruct((6, tiles * TILE), f32),
        in_specs=[SMEM, SMEM, SMEM, HBM, HBM, HBM, HBM, HBM],
        out_specs=VMEM,
        scratch_shapes=[
            pltpu.VMEM((2, num_slots), jnp.int32),
            pltpu.VMEM((3, tiles * TILE), f32),
            pltpu.VMEM((3, tiles * TILE), f32),
            pltpu.VMEM((tiles, TILE), f32),
            pltpu.VMEM((tiles, TILE), jnp.int32),
            pltpu.VMEM((tiles, 8, TILE), f32),
            pltpu.VMEM((nt, 8, TILE), f32),
            pltpu.VMEM((ns, 8, TILE), f32),
            pltpu.VMEM((nt, 7, TILE, TILE), f32),
            pltpu.VMEM((16, 4 * TILE), bf16),
            pltpu.VMEM((tiles, 16, TILE), f32),
            pltpu.VMEM((nt, 16, 2 * TILE), bf16),
            pltpu.VMEM((ns, 16, 2 * TILE), bf16),
            pltpu.VMEM((UNROLL, 2 * TILE, 2 * TILE), bf16),
            pltpu.VMEM((UNROLL, 2 * TILE, 2 * TILE), bf16),
            pltpu.VMEM((num_slots, 8, 2 * TILE), f32),
            pltpu.VMEM((num_slots, 8, 2 * TILE), f32),
            pltpu.VMEM((ncols, 6, tiles, TILE), f32),
            pltpu.VMEM((nrows, 6, tiles, TILE), f32),
            pltpu.VMEM((ncols - 1, 6, tiles, TILE), f32),
            pltpu.VMEM((nrows - 1, 6, tiles, TILE), f32),
            pltpu.SemaphoreType.DMA((5,)),
            pltpu.SemaphoreType.DMA((2, others)),
            pltpu.SemaphoreType.DMA((2, others)),
        ],
        compiler_params=pltpu.CompilerParams(
            collective_id=0, has_side_effects=True, vmem_limit_bytes=56 * 1024 * 1024
        ),
        name="wake",
    )(pair_slots, pair_count, tile_counts, pair_slots, positions, strengths,
      cores.reshape(tiles, TILE), order.reshape(tiles, TILE))
    return sums[0:3], sums[3:6]


def solution(mesh):
    whole = ("groups", "row", "col")
    in_specs = (P(None, whole), P(None, whole), P(whole), P(whole), P(whole), P(None, whole), P(whole))
    out_specs = (P(None, whole), P(None, whole))
    body = functools.partial(shards, mesh.shape["row"], mesh.shape["col"])
    return jax.shard_map(body, mesh=mesh, in_specs=in_specs, out_specs=out_specs, check_vma=False)
```
